32 devices in a mesh: tok: 8 (over z, core), cell: 4 (over y, x).
Axes of the slice: x: 2, y: 2, z: 4, core: 2. Of those that a mesh axis runs over, the one named last changes fastest.
Arguments:
- activations: bfloat16 [8192, 4096], P('tok'), may hold values from -6 to 6
- out_grads: bfloat16 [8192, 1024], P('tok'), may hold values from -6 to 6
- query_ids: int32 [8192], P('tok'), may hold values from 0 to 511
- live: int32 [8], P('tok'), may hold values from 256 to 1024, as said below
- proj_in: bfloat16 [4096, 64], P(None, 'cell'), may hold values from -0.09375 to 0.09375
- proj_out: bfloat16 [1024, 32], replicated, may hold values from -0.1875 to 0.1875
- whitener: bfloat16 [2048, 2048], P('cell')
- stores: bfloat16 [49152, 2048], P(('tok', 'cell')), may hold values from -0.023925781 to 0.023925781
Outputs:
- scores: float32 [512, 49152], P(None, ('tok', 'cell'))
The draws below stay inside these ranges and needn't reach their ends.
Inputs may be any that keep to these rules, and one draw needn't show every extreme that they name: `live`: each entry is a count of valid tokens of one block of 1024; some block is full in every draw.
All inputs are finite; a program needn't handle non-finite values.
Results may differ from the reference program's by a relative error of at most 0.005.
Values may be sent and summed in bfloat16 or wider, within the bound.
A program may use at most 64 MiB of HBM per device.

```python
import jax
import jax.numpy as jnp

D = 4096
KV = 1024
RA = 64
RB = 32
Q = 512
TOK_DEV = 1024
FEAT = 2048
TOKENS = 8192
STORES = 49152
N_TOK = 8


def draw_live(key, part):
    counts = jax.random.randint(key, (N_TOK,), TOK_DEV // 4, TOK_DEV + 1)
    full_block = jax.random.randint(jax.random.fold_in(key, 7), (), 0, N_TOK)
    return counts.at[full_block].set(TOK_DEV).astype(jnp.int32)


def draw_whitener(key, part):
    diag_key = jax.random.fold_in(key, 11)
    off_key = jax.random.fold_in(key, 13)
    diagonal = jnp.exp(jax.random.uniform(diag_key, (FEAT,), jnp.float32, jnp.log(0.3), jnp.log(3.0)))
    off_part = jax.random.normal(off_key, (FEAT, FEAT), jnp.float32) * (0.6 / FEAT ** 0.5)
    whole = jnp.diag(diagonal) + off_part
    return whole.astype(jnp.bfloat16)


def set_ends(result, own_key, low, largest):
    longest = result.shape.index(max(result.shape))
    spots = []
    for shift in (0, 1):
        where = [jax.random.randint(jax.random.fold_in(own_key, axis), (), 0, length) for axis, length in enumerate(result.shape)]
        where[longest] = (where[longest] + shift) % result.shape[longest]
        spots.append(tuple(where))
    return result.at[spots[0]].set(low).at[spots[1]].set(largest)


def level_of(key, extent, split, least, largest):
    loudness = 1.0
    for axis_at, parts in split:
        steps = jax.random.uniform(jax.random.fold_in(jax.random.fold_in(key, 6), axis_at), (parts,), jnp.float32, least / len(split), largest / len(split))
        loudness = loudness * jnp.repeat(jnp.exp(steps), extent[axis_at] // parts).reshape((-1,) + (1,) * (len(extent) - 1 - axis_at))
    return loudness


def bell_draw(key, dims, width, most, cuts=(), held_as=jnp.bfloat16):
    values = jax.random.normal(key, dims, jnp.float32) * width
    if len(cuts) > 0:
        values = level_of(key, dims, cuts, -0.22, 0.18) * values
    return jnp.clip(values, min=-most, max=most).astype(held_as)


def setup_inputs(seed: int = 0) -> dict:
    key_list = jax.random.split(jax.random.key(seed), 9)
    activations = bell_draw(key_list[0], (TOKENS, D), 1.0, 6.0, ((0, 8),))
    out_grads = bell_draw(key_list[1], (TOKENS, KV), 1.0, 6.0, ((0, 8),))
    query_ids = set_ends(jax.random.randint(key_list[2], (TOKENS,), 0, Q), jax.random.fold_in(key_list[2], 1), 0, Q - 1).astype(jnp.int32)
    live = draw_live(jax.random.fold_in(key_list[8], 71), 0)
    proj_in = bell_draw(key_list[4], (D, RA), D ** -0.5, 0.09375, ((1, 4),))
    proj_out = bell_draw(key_list[5], (KV, RB), KV ** -0.5, 0.1875)
    whitener = draw_whitener(jax.random.fold_in(key_list[8], 71), 0)
    stores = bell_draw(key_list[7], (STORES, FEAT), 0.004, 0.023925781, ((0, 32),))
    return {"activations": activations, "out_grads": out_grads, "query_ids": query_ids, "live": live, "proj_in": proj_in, "proj_out": proj_out, "whitener": whitener, "stores": stores}


def reference(activations, out_grads, query_ids, live, proj_in, proj_out, whitener, stores):
    token_count = activations.shape[0]
    positions = jnp.arange(token_count, dtype=jnp.int32)
    valid_mask = ((positions % TOK_DEV) < live[positions // TOK_DEV]).astype(jnp.float32)
    left_proj = jnp.dot(activations, proj_in, preferred_element_type=jnp.float32)
    right_proj = jnp.dot(out_grads, proj_out, preferred_element_type=jnp.float32)
    outer_cells = (left_proj[:, :, None] * right_proj[:, None, :] * valid_mask[:, None, None])
    outer_cells = outer_cells.reshape(token_count, RA * RB).astype(jnp.bfloat16)
    onehot = (query_ids[:, None] == jnp.arange(Q, dtype=jnp.int32)[None, :]).astype(jnp.bfloat16)
    summed = jnp.dot(onehot.T, outer_cells, preferred_element_type=jnp.float32).astype(jnp.bfloat16)
    whitened = jnp.dot(summed, whitener, preferred_element_type=jnp.float32).astype(jnp.bfloat16)
    return jnp.dot(whitened, stores.T, preferred_element_type=jnp.float32)
```

```python
import functools

import jax
import jax.numpy as jnp
from jax import lax
from jax.experimental import pallas as pl
from jax.experimental.pallas import tpu as pltpu
from jax.sharding import PartitionSpec as P

Q = 512
CORES = 2
MESH = pl.DeviceIdType.MESH
F32 = jnp.float32
BF16 = jnp.bfloat16


def tile_of(extent, most):
    size = min(extent, most)
    while extent % size:
        size //= 2
    return size


def dot(a, b):
    return jnp.dot(a, b, preferred_element_type=F32)


def spread(values, pattern):
    high = values.astype(BF16)
    low = (values - high.astype(F32)).astype(BF16)
    return dot(high, pattern) + dot(low, pattern)


def kernel(
    nt, nc, act_hbm, og_hbm, ids_ref, live_ref, pin_hbm, pout_ref, wh_hbm, st_hbm, out_ref,
    act, og, pin, wh, st, outer, hot, sib_out, sib_in, own, z_out, z_in, summed, c_out, c_in, own_w, gath,
    load_sem, sib_sem, z_sem, c_sem, gz_sem, gc_sem, gs_sem,
):
    tok = lax.axis_index("tok")
    cell = lax.axis_index("cell")
    nz = nt // CORES
    zz = tok // CORES
    core = tok % CORES
    toks, fc = outer.shape
    qb = Q // nt
    fw = wh.shape[2]
    ra, rb = pin.shape[1], pout_ref.shape[1]
    bits = nc.bit_length() - 1

    def cell_at(m):
        other = cell
        for k in range(bits):
            if m & (1 << k):
                other = other + (1 << k) * (1 - 2 * ((cell // (1 << k)) % 2))
        return other

    def z_at(j):
        return ((zz + j) % nz) * CORES + core

    def z_from(j):
        return ((zz + nz - j) % nz) * CORES

    sibling = zz * CORES + (1 - core)

    barrier = pltpu.get_barrier_semaphore()
    pl.semaphore_signal(barrier, inc=1, device_id={"tok": sibling}, device_id_type=MESH)
    for j in range(1, nz):
        pl.semaphore_signal(barrier, inc=1, device_id={"tok": z_at(j)}, device_id_type=MESH)
    for m in range(1, nc):
        pl.semaphore_signal(barrier, inc=1, device_id={"cell": cell_at(m)}, device_id_type=MESH)

    rows = tile_of(toks, 256)
    steps = toks // rows
    loads = []

    def load(src, dst):
        copy = pltpu.make_async_copy(src, dst, load_sem.at[len(loads)])
        copy.start()
        loads.append(copy)
        return copy

    pin_load = load(pin_hbm, pin)
    chunk_loads = []
    for s in range(steps):
        part = pl.ds(s * rows, rows)
        chunk_loads.append((load(og_hbm.at[part], og.at[part]), load(act_hbm.at[part], act.at[part])))
    wh_loads, st_loads = [], []
    for m in range(nc):
        cols = pl.ds(pl.multiple_of(cell_at(m) * fw, fw), fw)
        wh_loads.append(load(wh_hbm.at[:, cols], wh.at[m]))
    for m in range(nc):
        cols = pl.ds(pl.multiple_of(cell_at(m) * fw, fw), fw)
        st_loads.append(load(st_hbm.at[:, cols], st.at[m]))

    ids = ids_ref[...]
    valid = lax.broadcasted_iota(jnp.int32, (1, toks), 1) < live_ref[0]
    ids = jnp.where(valid, ids, -1)
    row = lax.broadcasted_iota(jnp.int32, (qb, toks), 0)
    for side in range(2):
        parity = 1 - core if side == 0 else core
        for j in range(nz):
            first = (((zz + j) % nz) * CORES + parity) * qb
            hot[side, pl.ds(j * qb, qb), :] = (row + first == ids).astype(F32).astype(BF16)

    feat = lax.broadcasted_iota(jnp.int32, (ra, fc), 1)
    at = lax.broadcasted_iota(jnp.int32, (ra, fc), 0)
    left_pat = ((feat >= at * rb) & (feat < at * rb + rb)).astype(F32).astype(BF16)
    feat = lax.broadcasted_iota(jnp.int32, (rb, fc), 1)
    at = lax.broadcasted_iota(jnp.int32, (rb, fc), 0)
    right_pat = (jnp.bitwise_and(feat, rb - 1) == at).astype(F32).astype(BF16)

    pin_load.wait()
    for s in range(steps):
        part = pl.ds(s * rows, rows)
        chunk_loads[s][0].wait()
        right = dot(og[part, :], pout_ref[...])
        chunk_loads[s][1].wait()
        left = dot(act[part, :], pin[...])
        outer[part, :] = (spread(left, left_pat) * spread(right, right_pat)).astype(BF16)

    sent = []

    def send(src, dst, sems, where):
        copy = pltpu.make_async_remote_copy(
            src_ref=src, dst_ref=dst, send_sem=sems.at[0], recv_sem=sems.at[1],
            device_id=where, device_id_type=MESH,
        )
        copy.start()
        sent.append(copy)

    def arrived(ref, sems, where):
        pltpu.make_async_remote_copy(
            src_ref=ref, dst_ref=ref, send_sem=sems.at[0], recv_sem=sems.at[1],
            device_id=where, device_id_type=MESH,
        ).wait_recv()

    to_sib = {"tok": sibling}

    z_order = [*range(1, nz), 0]
    theirs = dot(hot[0], outer[...]).astype(BF16)
    for j in range(nz):
        sib_out[j] = theirs[j * qb : (j + 1) * qb]
    pl.semaphore_wait(barrier, 1 + (nz - 1) + (nc - 1))
    for j in z_order:
        send(sib_out.at[j], sib_in.at[j], sib_sem.at[j], to_sib)
    mine = dot(hot[1], outer[...])
    for j in range(nz):
        own[j] = mine[j * qb : (j + 1) * qb]
    for j in z_order:
        arrived(sib_in.at[j], sib_sem.at[j], to_sib)
        both = own[j] + sib_in[j].astype(F32)
        if j:
            z_out[j] = both.astype(BF16)
            send(z_out.at[j], z_in.at[j], z_sem.at[j], {"tok": z_at(j)})
        else:
            own[0] = both
    total = own[0]
    for j in range(1, nz):
        arrived(z_in.at[j], z_sem.at[j], {"tok": z_at(j)})
        total = total + z_in[j].astype(F32)
    summed[...] = total.astype(BF16)

    for m in reversed(range(nc)):
        wh_loads[m].wait()
        product = dot(summed[...], wh[m])
        if m:
            c_out[m] = product.astype(BF16)
            send(c_out.at[m], c_in.at[m], c_sem.at[m], {"cell": cell_at(m)})
        else:
            own_w[...] = product
    total = own_w[...]
    for m in range(1, nc):
        arrived(c_in.at[m], c_sem.at[m], {"cell": cell_at(m)})
        total = total + c_in[m].astype(F32)
    gath[0, tok] = total.astype(BF16)

    half = qb // 2

    def order(m):
        return bin(m).count("1")

    slots = sorted(range(nc), key=order)

    def forward(s, j):
        at = z_from(j) + core
        for m in slots:
            if order(m) != order(s) + 1 or (m & s) != s:
                continue
            step = m ^ s
            where = {"cell": cell_at(step)}
            if order(m) == 1:
                send(gath.at[s, at], gath.at[m, at], gc_sem.at[m, j, 0], where)
                continue
            if step == 1 << (m.bit_length() - 1):
                part = pl.ds(0, half)
                send(gath.at[s, at, part], gath.at[m, at, part], gc_sem.at[m, j, 0], where)
            if step == m & -m:
                part = pl.ds(half, half)
                send(gath.at[s, at, part], gath.at[m, at, part], gc_sem.at[m, j, 1], where)
        send(gath.at[s, at], gath.at[s, at], gs_sem.at[s, j], to_sib)

    def take(m, j):
        at = z_from(j) + core
        if order(m) == 1:
            arrived(gath.at[m, at], gc_sem.at[m, j, 0], {"cell": cell_at(m)})
        else:
            for h, step in ((0, 1 << (m.bit_length() - 1)), (1, m & -m)):
                part = pl.ds(h * half, half)
                arrived(gath.at[m, at, part], gc_sem.at[m, j, h], {"cell": cell_at(step)})

    def multiply(m):
        for j in range(nz):
            at = z_from(j) + (1 - core)
            arrived(gath.at[m, at], gs_sem.at[m, j], to_sib)
        st_loads[m].wait()
        width = tile_of(out_ref.shape[1], 512)

        @pl.loop(0, out_ref.shape[1] // width)
        def _(n):
            cols = pl.ds(pl.multiple_of(n * width, width), width)
            piece = lax.dot_general(
                gath[m].reshape(Q, fw), st[m, cols, :], (((1,), (1,)), ((), ())), preferred_element_type=F32
            )
            if m == 0:
                out_ref[:, cols] = piece
            else:
                out_ref[:, cols] += piece

    for j in range(1, nz):
        send(gath.at[0, tok], gath.at[0, tok], gz_sem.at[j], {"tok": z_at(j)})
    forward(0, 0)
    ones = [m for m in slots if order(m) == 1]
    more = [m for m in slots if order(m) > 1]
    for j in range(1, nz):
        at = z_from(j) + core
        arrived(gath.at[0, at], gz_sem.at[j], {"tok": z_at(j)})
        forward(0, j)
        for m in ones:
            take(m, j - 1)
            forward(m, j - 1)
    multiply(0)
    for m in ones:
        take(m, nz - 1)
        forward(m, nz - 1)
    for n, m in enumerate(more):
        for j in range(nz):
            take(m, j)
            forward(m, j)
    for m in ones:
        multiply(m)
    for m in more:
        multiply(m)
    for copy in sent:
        copy.wait_send()


def shards(nt, nc, activations, out_grads, query_ids, live, proj_in, proj_out, whitener, stores):
    toks, d = activations.shape
    kv, rb = proj_out.shape
    ra = proj_in.shape[1]
    fc, feat = whitener.shape
    fw = feat // nc
    n_stores = stores.shape[0]
    nz = nt // CORES
    qb = Q // nt
    any_spec = pl.BlockSpec(memory_space=pl.ANY)
    vmem = pl.BlockSpec(memory_space=pltpu.VMEM)
    n_loads = 1 + 2 * (toks // tile_of(toks, 256)) + 2 * nc
    dma = pltpu.SemaphoreType.DMA
    return pl.pallas_call(
        functools.partial(kernel, nt, nc),
        out_shape=jax.ShapeDtypeStruct((Q, n_stores), F32),
        in_specs=[
            any_spec, any_spec, vmem, pl.BlockSpec(memory_space=pltpu.SMEM),
            any_spec, vmem, any_spec, any_spec,
        ],
        out_specs=vmem,
        scratch_shapes=[
            pltpu.VMEM((toks, d), BF16),
            pltpu.VMEM((toks, kv), BF16),
            pltpu.VMEM((d, ra), BF16),
            pltpu.VMEM((nc, fc, fw), BF16),
            pltpu.VMEM((nc, n_stores, fw), BF16),
            pltpu.VMEM((toks, fc), BF16),
            pltpu.VMEM((2, nz * qb, toks), BF16),
            pltpu.VMEM((nz, qb, fc), BF16),
            pltpu.VMEM((nz, qb, fc), BF16),
            pltpu.VMEM((nz, qb, fc), F32),
            pltpu.VMEM((nz, qb, fc), BF16),
            pltpu.VMEM((nz, qb, fc), BF16),
            pltpu.VMEM((qb, fc), BF16),
            pltpu.VMEM((nc, qb, fw), BF16),
            pltpu.VMEM((nc, qb, fw), BF16),
            pltpu.VMEM((qb, fw), F32),
            pltpu.VMEM((nc, nt, qb, fw), BF16),
            dma((n_loads,)),
            dma((nz, 2)),
            dma((nz, 2)),
            dma((nc, 2)),
            dma((nz, 2)),
            dma((nc, nz, 2, 2)),
            dma((nc, nz, 2)),
        ],
        compiler_params=pltpu.CompilerParams(
            collective_id=0, has_side_effects=True, vmem_limit_bytes=48 * 2**20
        ),
        cost_estimate=pl.CostEstimate(
            flops=2 * Q * n_stores * feat, bytes_accessed=24 * 2**20, transcendentals=0
        ),
        name="influence_scores",
    )(activations, out_grads, query_ids.reshape(1, toks), live, proj_in, proj_out, whitener, stores)


def solution(mesh):
    in_specs = (
        P("tok", None),
        P("tok", None),
        P("tok"),
        P("tok"),
        P(None, "cell"),
        P(),
        P("cell", None),
        P(("tok", "cell"), None),
    )
    out_specs = P(None, ("tok", "cell"))
    body = functools.partial(shards, mesh.shape["tok"], mesh.shape["cell"])
    return jax.shard_map(body, mesh=mesh, in_specs=in_specs, out_specs=out_specs, check_vma=False)
```

```python
import functools

import jax
import jax.numpy as jnp
from jax import lax
from jax.experimental import pallas as pl
from jax.experimental.pallas import tpu as pltpu
from jax.sharding import PartitionSpec as P

Q = 512
CORES = 2
MESH = pl.DeviceIdType.MESH
F32 = jnp.float32
BF16 = jnp.bfloat16


def tile_of(extent, most):
    size = min(extent, most)
    while extent % size:
        size //= 2
    return size


def dot(a, b):
    return jnp.dot(a, b, preferred_element_type=F32)


def dot_t(a, b):
    return lax.dot_general(a, b, (((1,), (1,)), ((), ())), preferred_element_type=F32)


def spread(values, pattern):
    high = values.astype(BF16)
    low = (values - high.astype(F32)).astype(BF16)
    return dot(high, pattern) + dot(low, pattern)


def kernel(
    nt, nc, act_hbm, og_hbm, ids_hbm, live_ref, pin_hbm, pout_hbm, wh_hbm, st_hbm, out_ref,
    act, og, ids_ref, pin, pout, wh, st, outer, hot, sib_out, sib_in, own, z_out, z_in, summed, c_out, c_in, own_w, gath,
    load_sem, sib_sem, z_sem, c_sem, gz_sem, gc_sem, gs_sem,
):
    tok = lax.axis_index("tok")
    cell = lax.axis_index("cell")
    nz = nt // CORES
    zz = tok // CORES
    core = tok % CORES
    toks, fc = outer.shape
    qb = Q // nt
    fw = wh.shape[2]
    ra, rb = pin.shape[0], pout.shape[0]
    bits = nc.bit_length() - 1

    def cell_at(m):
        other = cell
        for k in range(bits):
            if m & (1 << k):
                other = other + (1 << k) * (1 - 2 * ((cell // (1 << k)) % 2))
        return other

    def z_at(j):
        return ((zz + j) % nz) * CORES + core

    def z_from(j):
        return ((zz + nz - j) % nz) * CORES

    sibling = zz * CORES + (1 - core)

    barrier = pltpu.get_barrier_semaphore()
    pl.semaphore_signal(barrier, inc=1, device_id={"tok": sibling}, device_id_type=MESH)
    for j in range(1, nz):
        pl.semaphore_signal(barrier, inc=1, device_id={"tok": z_at(j)}, device_id_type=MESH)
    for m in range(1, nc):
        pl.semaphore_signal(barrier, inc=1, device_id={"cell": cell_at(m)}, device_id_type=MESH)

    rows = tile_of(toks, 256)
    steps = toks // rows
    loads = []

    def load(src, dst):
        copy = pltpu.make_async_copy(src, dst, load_sem.at[len(loads)])
        copy.start()
        loads.append(copy)
        return copy

    ids_load = load(ids_hbm, ids_ref)
    pin_load = load(pin_hbm, pin)
    pout_load = load(pout_hbm, pout)
    chunk_loads = []
    for s in range(steps):
        part = pl.ds(s * rows, rows)
        chunk_loads.append((load(og_hbm.at[part], og.at[part]), load(act_hbm.at[part], act.at[part])))
    wh_loads, st_loads = [], []
    for m in range(nc):
        cols = pl.ds(pl.multiple_of(cell_at(m) * fw, fw), fw)
        wh_loads.append(load(wh_hbm.at[:, cols], wh.at[m]))

    ids_load.wait()
    ids = ids_ref[...]
    valid = lax.broadcasted_iota(jnp.int32, (1, toks), 1) < live_ref[0]
    ids = jnp.where(valid, ids, -1)
    row = lax.broadcasted_iota(jnp.int32, (qb, toks), 0)
    for side in range(2):
        parity = 1 - core if side == 0 else core
        for j in range(nz):
            first = (((zz + j) % nz) * CORES + parity) * qb
            hot[side, pl.ds(j * qb, qb), :] = (row + first == ids).astype(F32).astype(BF16)

    feat = lax.broadcasted_iota(jnp.int32, (ra, fc), 1)
    at = lax.broadcasted_iota(jnp.int32, (ra, fc), 0)
    left_pat = ((feat >= at * rb) & (feat < at * rb + rb)).astype(F32).astype(BF16)
    feat = lax.broadcasted_iota(jnp.int32, (rb, fc), 1)
    at = lax.broadcasted_iota(jnp.int32, (rb, fc), 0)
    right_pat = (jnp.bitwise_and(feat, rb - 1) == at).astype(F32).astype(BF16)

    pin_load.wait()
    pout_load.wait()
    for s in range(steps):
        part = pl.ds(s * rows, rows)
        chunk_loads[s][0].wait()
        right = dot_t(og[part, :], pout[...])
        chunk_loads[s][1].wait()
        left = dot_t(act[part, :], pin[...])
        outer[part, :] = (spread(left, left_pat) * spread(right, right_pat)).astype(BF16)

    for m in range(nc):
        cols = pl.ds(pl.multiple_of(cell_at(m) * fw, fw), fw)
        st_loads.append(load(st_hbm.at[:, cols], st.at[m]))

    sent = []

    def send(src, dst, sems, where):
        copy = pltpu.make_async_remote_copy(
            src_ref=src, dst_ref=dst, send_sem=sems.at[0], recv_sem=sems.at[1],
            device_id=where, device_id_type=MESH,
        )
        copy.start()
        sent.append(copy)

    def arrived(ref, sems, where):
        pltpu.make_async_remote_copy(
            src_ref=ref, dst_ref=ref, send_sem=sems.at[0], recv_sem=sems.at[1],
            device_id=where, device_id_type=MESH,
        ).wait_recv()

    to_sib = {"tok": sibling}

    z_order = [*range(1, nz), 0]
    theirs = dot(hot[0], outer[...]).astype(BF16)
    for j in range(nz):
        sib_out[j] = theirs[j * qb : (j + 1) * qb]
    pl.semaphore_wait(barrier, 1 + (nz - 1) + (nc - 1))
    for j in z_order:
        send(sib_out.at[j], sib_in.at[j], sib_sem.at[j], to_sib)
    mine = dot(hot[1], outer[...])
    for j in range(nz):
        own[j] = mine[j * qb : (j + 1) * qb]
    for j in z_order:
        arrived(sib_in.at[j], sib_sem.at[j], to_sib)
        both = own[j] + sib_in[j].astype(F32)
        if j:
            z_out[j] = both.astype(BF16)
            send(z_out.at[j], z_in.at[j], z_sem.at[j], {"tok": z_at(j)})
        else:
            own[0] = both
    total = own[0]
    for j in range(1, nz):
        arrived(z_in.at[j], z_sem.at[j], {"tok": z_at(j)})
        total = total + z_in[j].astype(F32)
    summed[...] = total.astype(BF16)

    for m in reversed(range(nc)):
        wh_loads[m].wait()
        product = dot(summed[...], wh[m])
        if m:
            c_out[m] = product.astype(BF16)
            send(c_out.at[m], c_in.at[m], c_sem.at[m], {"cell": cell_at(m)})
        else:
            own_w[...] = product
    total = own_w[...]
    for m in range(1, nc):
        arrived(c_in.at[m], c_sem.at[m], {"cell": cell_at(m)})
        total = total + c_in[m].astype(F32)
    gath[0, tok] = total.astype(BF16)

    half = qb // 2

    def order(m):
        return bin(m).count("1")

    slots = sorted(range(nc), key=order)

    def forward(s, j):
        at = z_from(j) + core
        for m in slots:
            if order(m) != order(s) + 1 or (m & s) != s:
                continue
            step = m ^ s
            where = {"cell": cell_at(step)}
            if order(m) == 1:
                send(gath.at[s, at], gath.at[m, at], gc_sem.at[m, j, 0], where)
                continue
            if step == 1 << (m.bit_length() - 1):
                part = pl.ds(0, half)
                send(gath.at[s, at, part], gath.at[m, at, part], gc_sem.at[m, j, 0], where)
            if step == m & -m:
                part = pl.ds(half, half)
                send(gath.at[s, at, part], gath.at[m, at, part], gc_sem.at[m, j, 1], where)
        send(gath.at[s, at], gath.at[s, at], gs_sem.at[s, j], to_sib)

    def take(m, j):
        at = z_from(j) + core
        if order(m) == 1:
            arrived(gath.at[m, at], gc_sem.at[m, j, 0], {"cell": cell_at(m)})
        else:
            for h, step in ((0, 1 << (m.bit_length() - 1)), (1, m & -m)):
                part = pl.ds(h * half, half)
                arrived(gath.at[m, at, part], gc_sem.at[m, j, h], {"cell": cell_at(step)})

    def multiply(m):
        for j in range(nz):
            at = z_from(j) + (1 - core)
            arrived(gath.at[m, at], gs_sem.at[m, j], to_sib)
        st_loads[m].wait()
        width = tile_of(out_ref.shape[1], 512)

        @pl.loop(0, out_ref.shape[1] // width)
        def _(n):
            cols = pl.ds(pl.multiple_of(n * width, width), width)
            piece = dot_t(gath[m].reshape(Q, fw), st[m, cols, :])
            if m == 0:
                out_ref[:, cols] = piece
            else:
                out_ref[:, cols] += piece

    for j in range(1, nz):
        send(gath.at[0, tok], gath.at[0, tok], gz_sem.at[j], {"tok": z_at(j)})
    forward(0, 0)
    ones = [m for m in slots if order(m) == 1]
    more = [m for m in slots if order(m) > 1]
    for j in range(1, nz):
        at = z_from(j) + core
        arrived(gath.at[0, at], gz_sem.at[j], {"tok": z_at(j)})
        forward(0, j)
        for m in ones:
            take(m, j - 1)
            forward(m, j - 1)
    multiply(0)
    for m in ones:
        take(m, nz - 1)
        forward(m, nz - 1)
    todo = list(ones)
    for m in more:
        for j in range(nz):
            take(m, j)
            forward(m, j)
            if todo and j >= nz // 2 - 1 and j < nz - 1:
                multiply(todo.pop(0))
        todo.append(m)
    for m in todo:
        multiply(m)
    for copy in sent:
        copy.wait_send()


def shards(nt, nc, activations, out_grads, query_ids, live, proj_in, proj_out, whitener, stores):
    toks, d = activations.shape
    kv, rb = proj_out.shape
    ra = proj_in.shape[1]
    fc, feat = whitener.shape
    fw = feat // nc
    n_stores = stores.shape[0]
    nz = nt // CORES
    qb = Q // nt
    hbm = pl.BlockSpec(memory_space=pltpu.HBM)
    vmem = pl.BlockSpec(memory_space=pltpu.VMEM)
    n_loads = 3 + 2 * (toks // tile_of(toks, 256)) + 2 * nc
    dma = pltpu.SemaphoreType.DMA
    return pl.pallas_call(
        functools.partial(kernel, nt, nc),
        out_shape=pltpu.VMEM((Q, n_stores), F32),
        in_specs=[
            hbm, hbm, hbm, pl.BlockSpec(memory_space=pltpu.SMEM),
            hbm, hbm, hbm, hbm,
        ],
        out_specs=vmem,
        scratch_shapes=[
            pltpu.VMEM((toks, d), BF16),
            pltpu.VMEM((toks, kv), BF16),
            pltpu.VMEM((1, toks), jnp.int32),
            pltpu.VMEM((ra, d), BF16),
            pltpu.VMEM((rb, kv), BF16),
            pltpu.VMEM((nc, fc, fw), BF16),
            pltpu.VMEM((nc, n_stores, fw), BF16),
            pltpu.VMEM((toks, fc), BF16),
            pltpu.VMEM((2, nz * qb, toks), BF16),
            pltpu.VMEM((nz, qb, fc), BF16),
            pltpu.VMEM((nz, qb, fc), BF16),
            pltpu.VMEM((nz, qb, fc), F32),
            pltpu.VMEM((nz, qb, fc), BF16),
            pltpu.VMEM((nz, qb, fc), BF16),
            pltpu.VMEM((qb, fc), BF16),
            pltpu.VMEM((nc, qb, fw), BF16),
            pltpu.VMEM((nc, qb, fw), BF16),
            pltpu.VMEM((qb, fw), F32),
            pltpu.VMEM((nc, nt, qb, fw), BF16),
            dma((n_loads,)),
            dma((nz, 2)),
            dma((nz, 2)),
            dma((nc, 2)),
            dma((nz, 2)),
            dma((nc, nz, 2, 2)),
            dma((nc, nz, 2)),
        ],
        compiler_params=pltpu.CompilerParams(
            collective_id=0, has_side_effects=True, vmem_limit_bytes=60 * 2**20
        ),
        cost_estimate=pl.CostEstimate(
            flops=2 * Q * n_stores * feat, bytes_accessed=24 * 2**20, transcendentals=0
        ),
        name="influence_scores",
    )(activations, out_grads, query_ids.reshape(1, toks), live, proj_in.T, proj_out.T, whitener, stores)


def solution(mesh):
    in_specs = (
        P("tok", None),
        P("tok", None),
        P("tok"),
        P("tok"),
        P(None, "cell"),
        P(),
        P("cell", None),
        P(("tok", "cell"), None),
    )
    out_specs = P(None, ("tok", "cell"))
    body = functools.partial(shards, mesh.shape["tok"], mesh.shape["cell"])
    return jax.shard_map(body, mesh=mesh, in_specs=in_specs, out_specs=out_specs, check_vma=False)
```

```python
import functools

import jax
import jax.numpy as jnp
from jax import lax
from jax.experimental import pallas as pl
from jax.experimental.pallas import tpu as pltpu
from jax.sharding import PartitionSpec as P

Q = 512
CORES = 2
MESH = pl.DeviceIdType.MESH
F32 = jnp.float32
BF16 = jnp.bfloat16


def tile_of(extent, most):
    size = min(extent, most)
    while extent % size:
        size //= 2
    return size


def dot(a, b):
    return jnp.dot(a, b, preferred_element_type=F32)


def dot_t(a, b):
    return lax.dot_general(a, b, (((1,), (1,)), ((), ())), preferred_element_type=F32)


def spread(twice, pattern):
    high = twice.astype(BF16).astype(F32)
    lane = lax.broadcasted_iota(jnp.int32, twice.shape, 1)
    return dot(jnp.where(lane < twice.shape[1] // 2, high, twice - high).astype(BF16), pattern)


def flipped(index, m):
    other = index
    for k in range(m.bit_length()):
        if m & (1 << k):
            other = other + (1 << k) * (1 - 2 * ((index // (1 << k)) % 2))
    return other


def kernel(
    nt, nc, act_hbm, og_hbm, ids_hbm, live_ref, pin_hbm, pout_hbm, wh_hbm, st_hbm, out_ref,
    act, og, ids_ref, pin, pout, wh, st, outer, hot, sib_out, sib_in, own, z_out, z_in, summed, c_out, c_in, own_w, gath,
    load_sem, sib_sem, z_sem, c_sem, gz_sem, gc_sem, gs_sem,
):
    tok = lax.axis_index("tok")
    cell = lax.axis_index("cell")
    nz = nt // CORES
    zz = tok // CORES
    core = tok % CORES
    toks, fc = outer.shape
    qb = Q // nt
    fw = wh.shape[2]
    ra, rb = pin.shape[1], pout.shape[1]

    def cell_at(m):
        return flipped(cell, m)

    def z_at(j):
        return flipped(zz, j) * CORES + core

    sibling = zz * CORES + (1 - core)

    barrier = pltpu.get_barrier_semaphore()
    pl.semaphore_signal(barrier, inc=1, device_id={"tok": sibling}, device_id_type=MESH)
    for j in range(1, nz):
        pl.semaphore_signal(barrier, inc=1, device_id={"tok": z_at(j)}, device_id_type=MESH)
    for m in range(1, nc):
        pl.semaphore_signal(barrier, inc=1, device_id={"cell": cell_at(m)}, device_id_type=MESH)

    rows = tile_of(toks, 256)
    steps = toks // rows
    loads = []

    def load(src, dst):
        copy = pltpu.make_async_copy(src, dst, load_sem.at[len(loads)])
        copy.start()
        loads.append(copy)
        return copy

    ids_load = load(ids_hbm, ids_ref)
    small_loads = [load(src, dst.at[n]) for src, dst in ((pin_hbm, pin), (pout_hbm, pout)) for n in range(2)]
    chunk_loads = []
    for s in range(steps):
        part = pl.ds(s * rows, rows)
        chunk_loads.append((load(og_hbm.at[part], og.at[part]), load(act_hbm.at[part], act.at[part])))
    wh_loads, st_loads = [], []
    for m in range(nc):
        cols = pl.ds(pl.multiple_of(cell_at(m) * fw, fw), fw)
        wh_loads.append(load(wh_hbm.at[:, cols], wh.at[m]))

    ids_load.wait()
    ids = ids_ref[...]
    valid = lax.broadcasted_iota(jnp.int32, (1, toks), 1) < live_ref[0]
    ids = jnp.where(valid, ids, -1)
    row = lax.broadcasted_iota(jnp.int32, (qb, toks), 0)
    for side in range(2):
        parity = 1 - core if side == 0 else core
        for j in range(nz):
            first = (flipped(zz, j) * CORES + parity) * qb
            hot[side, pl.ds(j * qb, qb), :] = (row + first == ids).astype(F32).astype(BF16)

    def pattern(n, test):
        feat = lax.broadcasted_iota(jnp.int32, (2 * n, fc), 1)
        at = lax.broadcasted_iota(jnp.int32, (2 * n, fc), 0)
        return test(feat, jnp.where(at < n, at, at - n)).astype(F32).astype(BF16)

    left_pat = pattern(ra, lambda feat, at: (feat >= at * rb) & (feat < at * rb + rb))
    right_pat = pattern(rb, lambda feat, at: jnp.bitwise_and(feat, rb - 1) == at)

    for copy in small_loads:
        copy.wait()
    pin_twice = pin[...].reshape(2 * ra, pin.shape[2])
    pout_twice = pout[...].reshape(2 * rb, pout.shape[2])
    for s in range(steps):
        part = pl.ds(s * rows, rows)
        chunk_loads[s][0].wait()
        right = dot_t(og[part, :], pout_twice)
        chunk_loads[s][1].wait()
        left = dot_t(act[part, :], pin_twice)
        outer[part, :] = (spread(left, left_pat) * spread(right, right_pat)).astype(BF16)

    for m in range(nc):
        cols = pl.ds(pl.multiple_of(cell_at(m) * fw, fw), fw)
        st_loads.append(load(st_hbm.at[:, cols], st.at[m]))

    sent = []

    def send(src, dst, sems, where):
        copy = pltpu.make_async_remote_copy(
            src_ref=src, dst_ref=dst, send_sem=sems.at[0], recv_sem=sems.at[1],
            device_id=where, device_id_type=MESH,
        )
        copy.start()
        sent.append(copy)

    def arrived(ref, sems, where):
        pltpu.make_async_remote_copy(
            src_ref=ref, dst_ref=ref, send_sem=sems.at[0], recv_sem=sems.at[1],
            device_id=where, device_id_type=MESH,
        ).wait_recv()

    to_sib = {"tok": sibling}

    z_order = [*range(1, nz), 0]
    theirs = dot(hot[0], outer[...]).astype(BF16)
    for j in range(nz):
        sib_out[j] = theirs[j * qb : (j + 1) * qb]
    pl.semaphore_wait(barrier, 1 + (nz - 1) + (nc - 1))
    for j in z_order:
        send(sib_out.at[j], sib_in.at[j], sib_sem.at[j], to_sib)
    mine = dot(hot[1], outer[...])
    for j in range(nz):
        own[j] = mine[j * qb : (j + 1) * qb]
    for j in z_order:
        arrived(sib_in.at[j], sib_sem.at[j], to_sib)
        both = own[j] + sib_in[j].astype(F32)
        if j:
            z_out[j] = both.astype(BF16)
            send(z_out.at[j], z_in.at[j], z_sem.at[j], {"tok": z_at(j)})
        else:
            own[0] = both
    total = own[0]
    for j in range(1, nz):
        arrived(z_in.at[j], z_sem.at[j], {"tok": z_at(j)})
        total = total + z_in[j].astype(F32)
    summed[...] = total.astype(BF16)

    for m in reversed(range(nc)):
        wh_loads[m].wait()
        product = dot(summed[...], wh[m])
        if m:
            c_out[m] = product.astype(BF16)
            send(c_out.at[m], c_in.at[m], c_sem.at[m], {"cell": cell_at(m)})
        else:
            own_w[...] = product
    total = own_w[...]
    for m in range(1, nc):
        arrived(c_in.at[m], c_sem.at[m], {"cell": cell_at(m)})
        total = total + c_in[m].astype(F32)
    gath[0, tok] = total.astype(BF16)

    half = qb // 2

    def order(m):
        return bin(m).count("1")

    slots = sorted(range(nc), key=order)

    def forward(s, j):
        at = z_at(j)
        for m in slots:
            if order(m) != order(s) + 1 or (m & s) != s:
                continue
            step = m ^ s
            where = {"cell": cell_at(step)}
            if order(m) == 1:
                send(gath.at[s, at], gath.at[m, at], gc_sem.at[m, j, 0], where)
                continue
            if step == 1 << (m.bit_length() - 1):
                part = pl.ds(0, half)
                send(gath.at[s, at, part], gath.at[m, at, part], gc_sem.at[m, j, 0], where)
            if step == m & -m:
                part = pl.ds(half, half)
                send(gath.at[s, at, part], gath.at[m, at, part], gc_sem.at[m, j, 1], where)
        send(gath.at[s, at], gath.at[s, at], gs_sem.at[s, j], to_sib)

    def take(m, j):
        at = z_at(j)
        if order(m) == 1:
            arrived(gath.at[m, at], gc_sem.at[m, j, 0], {"cell": cell_at(m)})
        else:
            for h, step in ((0, 1 << (m.bit_length() - 1)), (1, m & -m)):
                part = pl.ds(h * half, half)
                arrived(gath.at[m, at, part], gc_sem.at[m, j, h], {"cell": cell_at(step)})

    def multiply(m):
        for j in range(nz):
            at = z_at(j) + 1 - 2 * core
            arrived(gath.at[m, at], gs_sem.at[m, j], to_sib)
        st_loads[m].wait()
        width = tile_of(out_ref.shape[1], 512)

        @pl.loop(0, out_ref.shape[1] // width)
        def _(n):
            cols = pl.ds(pl.multiple_of(n * width, width), width)
            piece = dot_t(gath[m].reshape(Q, fw), st[m, cols, :])
            if m == 0:
                out_ref[:, cols] = piece
            else:
                out_ref[:, cols] += piece

    for j in range(1, nz):
        send(gath.at[0, tok], gath.at[0, tok], gz_sem.at[j], {"tok": z_at(j)})
    forward(0, 0)
    ones = [m for m in slots if order(m) == 1]
    more = [m for m in slots if order(m) > 1]
    for j in range(1, nz):
        for m in ones:
            take(m, j - 1)
            forward(m, j - 1)
        at = z_at(j)
        arrived(gath.at[0, at], gz_sem.at[j], {"tok": at})
        forward(0, j)
    for m in ones:
        take(m, nz - 1)
        forward(m, nz - 1)
    todo = [0, *ones]
    for m in more:
        for j in range(nz):
            take(m, j)
            forward(m, j)
            if todo and j >= nz // 2 - 1 and j < nz - 1:
                multiply(todo.pop(0))
        todo.append(m)
    for m in todo:
        multiply(m)
    for copy in sent:
        copy.wait_send()


def shards(nt, nc, activations, out_grads, query_ids, live, proj_in, proj_out, whitener, stores):
    toks, d = activations.shape
    kv, rb = proj_out.shape
    ra = proj_in.shape[1]
    fc, feat = whitener.shape
    fw = feat // nc
    n_stores = stores.shape[0]
    nz = nt // CORES
    qb = Q // nt
    hbm = pl.BlockSpec(memory_space=pltpu.HBM)
    vmem = pl.BlockSpec(memory_space=pltpu.VMEM)
    n_loads = 5 + 2 * (toks // tile_of(toks, 256)) + 2 * nc
    dma = pltpu.SemaphoreType.DMA
    return pl.pallas_call(
        functools.partial(kernel, nt, nc),
        out_shape=pltpu.VMEM((Q, n_stores), F32),
        in_specs=[
            hbm, hbm, hbm, pl.BlockSpec(memory_space=pltpu.SMEM),
            hbm, hbm, hbm, hbm,
        ],
        out_specs=vmem,
        scratch_shapes=[
            pltpu.VMEM((toks, d), BF16),
            pltpu.VMEM((toks, kv), BF16),
            pltpu.VMEM((1, toks), jnp.int32),
            pltpu.VMEM((2, ra, d), BF16),
            pltpu.VMEM((2, rb, kv), BF16),
            pltpu.VMEM((nc, fc, fw), BF16),
            pltpu.VMEM((nc, n_stores, fw), BF16),
            pltpu.VMEM((toks, fc), BF16),
            pltpu.VMEM((2, nz * qb, toks), BF16),
            pltpu.VMEM((nz, qb, fc), BF16),
            pltpu.VMEM((nz, qb, fc), BF16),
            pltpu.VMEM((nz, qb, fc), F32),
            pltpu.VMEM((nz, qb, fc), BF16),
            pltpu.VMEM((nz, qb, fc), BF16),
            pltpu.VMEM((qb, fc), BF16),
            pltpu.VMEM((nc, qb, fw), BF16),
            pltpu.VMEM((nc, qb, fw), BF16),
            pltpu.VMEM((qb, fw), F32),
            pltpu.VMEM((nc, nt, qb, fw), BF16),
            dma((n_loads,)),
            dma((nz, 2)),
            dma((nz, 2)),
            dma((nc, 2)),
            dma((nz, 2)),
            dma((nc, nz, 2, 2)),
            dma((nc, nz, 2)),
        ],
        compiler_params=pltpu.CompilerParams(
            collective_id=0, has_side_effects=True, vmem_limit_bytes=60 * 2**20
        ),
        cost_estimate=pl.CostEstimate(
            flops=2 * Q * n_stores * feat, bytes_accessed=24 * 2**20, transcendentals=0
        ),
        name="influence_scores",
    )(activations, out_grads, query_ids.reshape(1, toks), live, proj_in.T, proj_out.T, whitener, stores)


def solution(mesh):
    in_specs = (
        P("tok", None),
        P("tok", None),
        P("tok"),
        P("tok"),
        P(None, "cell"),
        P(),
        P("cell", None),
        P(("tok", "cell"), None),
    )
    out_specs = P(None, ("tok", "cell"))
    body = functools.partial(shards, mesh.shape["tok"], mesh.shape["cell"])
    return jax.shard_map(body, mesh=mesh, in_specs=in_specs, out_specs=out_specs, check_vma=False)
```

```python
import functools

import jax
import jax.numpy as jnp
from jax import lax
from jax.experimental import pallas as pl
from jax.experimental.pallas import tpu as pltpu
from jax.sharding import PartitionSpec as P

Q = 512
CORES = 2
MESH = pl.DeviceIdType.MESH
F32 = jnp.float32
BF16 = jnp.bfloat16


def tile_of(extent, most):
    size = min(extent, most)
    while extent % size:
        size //= 2
    return size


def dot(a, b):
    return jnp.dot(a, b, preferred_element_type=F32)


def dot_t(a, b):
    return lax.dot_general(a, b, (((1,), (1,)), ((), ())), preferred_element_type=F32)


def spread(twice, pattern):
    high = twice.astype(BF16).astype(F32)
    lane = lax.broadcasted_iota(jnp.int32, twice.shape, 1)
    return dot(jnp.where(lane < twice.shape[1] // 2, high, twice - high).astype(BF16), pattern)


def flipped(index, m):
    other = index
    for k in range(m.bit_length()):
        if m & (1 << k):
            other = other + (1 << k) * (1 - 2 * ((index // (1 << k)) % 2))
    return other


def kernel(
    nt, nc, act_hbm, og_hbm, ids_hbm, live_ref, pin_hbm, pout_hbm, wh_hbm, st_hbm, out_ref,
    act, og, ids_ref, pin, pout, wh, st, outer, hot, sib_out, sib_in, own, z_out, z_in, summed, c_out, c_in, own_w, gath,
    load_sem, sib_sem, z_sem, c_sem, gz_sem, gc_sem, gs_sem,
):
    tok = lax.axis_index("tok")
    cell = lax.axis_index("cell")
    nz = nt // CORES
    zz = tok // CORES
    core = tok % CORES
    toks, fc = outer.shape
    qb = Q // nt
    fw = wh.shape[2]
    ra, rb = pin.shape[1], pout.shape[1]

    def cell_at(m):
        return flipped(cell, m)

    def z_at(j):
        return flipped(zz, j) * CORES + core

    sibling = zz * CORES + (1 - core)

    barrier = pltpu.get_barrier_semaphore()
    pl.semaphore_signal(barrier, inc=1, device_id={"tok": sibling}, device_id_type=MESH)
    for j in range(1, nz):
        pl.semaphore_signal(barrier, inc=1, device_id={"tok": z_at(j)}, device_id_type=MESH)
    for m in range(1, nc):
        pl.semaphore_signal(barrier, inc=1, device_id={"cell": cell_at(m)}, device_id_type=MESH)

    rows = tile_of(toks, 256)
    steps = toks // rows
    loads = []

    def load(src, dst):
        copy = pltpu.make_async_copy(src, dst, load_sem.at[len(loads)])
        copy.start()
        loads.append(copy)
        return copy

    ids_load = load(ids_hbm, ids_ref)
    small_loads = [load(src, dst.at[n]) for src, dst in ((pin_hbm, pin), (pout_hbm, pout)) for n in range(2)]
    chunk_loads = []
    for s in range(steps):
        part = pl.ds(s * rows, rows)
        chunk_loads.append((load(og_hbm.at[part], og.at[part]), load(act_hbm.at[part], act.at[part])))
    wh_loads, st_loads = [], []
    for m in range(nc):
        cols = pl.ds(pl.multiple_of(cell_at(m) * fw, fw), fw)
        wh_loads.append(load(wh_hbm.at[:, cols], wh.at[m]))

    ids_load.wait()
    ids = ids_ref[...]
    valid = lax.broadcasted_iota(jnp.int32, (1, toks), 1) < live_ref[0]
    ids = jnp.where(valid, ids, -1)
    row = lax.broadcasted_iota(jnp.int32, (qb, toks), 0)
    for side in range(2):
        parity = 1 - core if side == 0 else core
        for j in range(nz):
            first = (flipped(zz, j) * CORES + parity) * qb
            hot[side, pl.ds(j * qb, qb), :] = (row + first == ids).astype(F32).astype(BF16)

    def pattern(n, test):
        feat = lax.broadcasted_iota(jnp.int32, (2 * n, fc), 1)
        at = lax.broadcasted_iota(jnp.int32, (2 * n, fc), 0)
        return test(feat, jnp.where(at < n, at, at - n)).astype(F32).astype(BF16)

    left_pat = pattern(ra, lambda feat, at: (feat >= at * rb) & (feat < at * rb + rb))
    right_pat = pattern(rb, lambda feat, at: jnp.bitwise_and(feat, rb - 1) == at)

    for copy in small_loads:
        copy.wait()
    pin_twice = pin[...].reshape(2 * ra, pin.shape[2])
    pout_twice = pout[...].reshape(2 * rb, pout.shape[2])
    for s in range(steps):
        part = pl.ds(s * rows, rows)
        chunk_loads[s][0].wait()
        right = dot_t(og[part, :], pout_twice)
        chunk_loads[s][1].wait()
        left = dot_t(act[part, :], pin_twice)
        outer[part, :] = (spread(left, left_pat) * spread(right, right_pat)).astype(BF16)

    for m in range(nc):
        cols = pl.ds(pl.multiple_of(cell_at(m) * fw, fw), fw)
        st_loads.append(load(st_hbm.at[:, cols], st.at[m]))

    sent = []

    def send(src, dst, sems, where):
        copy = pltpu.make_async_remote_copy(
            src_ref=src, dst_ref=dst, send_sem=sems.at[0], recv_sem=sems.at[1],
            device_id=where, device_id_type=MESH,
        )
        copy.start()
        sent.append(copy)

    def arrived(ref, sems, where):
        pltpu.make_async_remote_copy(
            src_ref=ref, dst_ref=ref, send_sem=sems.at[0], recv_sem=sems.at[1],
            device_id=where, device_id_type=MESH,
        ).wait_recv()

    to_sib = {"tok": sibling}

    z_order = [*range(1, nz), 0]
    theirs = dot(hot[0], outer[...]).astype(BF16)
    for j in range(nz):
        sib_out[j] = theirs[j * qb : (j + 1) * qb]
    pl.semaphore_wait(barrier, 1 + (nz - 1) + (nc - 1))
    for j in z_order:
        send(sib_out.at[j], sib_in.at[j], sib_sem.at[j], to_sib)
    mine = dot(hot[1], outer[...])
    for j in range(nz):
        own[j] = mine[j * qb : (j + 1) * qb]
    for j in z_order:
        arrived(sib_in.at[j], sib_sem.at[j], to_sib)
        both = own[j] + sib_in[j].astype(F32)
        if j:
            z_out[j] = both.astype(BF16)
            send(z_out.at[j], z_in.at[j], z_sem.at[j], {"tok": z_at(j)})
        else:
            own[0] = both
    total = own[0]
    for j in range(1, nz):
        arrived(z_in.at[j], z_sem.at[j], {"tok": z_at(j)})
        total = total + z_in[j].astype(F32)
    summed[...] = total.astype(BF16)

    for m in reversed(range(nc)):
        wh_loads[m].wait()
        product = dot(summed[...], wh[m])
        if m:
            c_out[m] = product.astype(BF16)
            send(c_out.at[m], c_in.at[m], c_sem.at[m], {"cell": cell_at(m)})
        else:
            own_w[...] = product
    total = own_w[...]
    for m in range(1, nc):
        arrived(c_in.at[m], c_sem.at[m], {"cell": cell_at(m)})
        total = total + c_in[m].astype(F32)
    gath[0, tok] = total.astype(BF16)

    half = qb // 2

    def order(m):
        return bin(m).count("1")

    slots = sorted(range(nc), key=order)

    def forward(s, j):
        at = z_at(j)
        for m in slots:
            if order(m) != order(s) + 1 or (m & s) != s:
                continue
            step = m ^ s
            where = {"cell": cell_at(step)}
            if order(m) == 1:
                send(gath.at[s, at], gath.at[m, at], gc_sem.at[m, j, 0], where)
                continue
            if step == 1 << (m.bit_length() - 1):
                part = pl.ds(0, half)
                send(gath.at[s, at, part], gath.at[m, at, part], gc_sem.at[m, j, 0], where)
            if step == m & -m:
                part = pl.ds(half, half)
                send(gath.at[s, at, part], gath.at[m, at, part], gc_sem.at[m, j, 1], where)
        send(gath.at[s, at], gath.at[s, at], gs_sem.at[s, j], to_sib)

    def take(m, j):
        at = z_at(j)
        if order(m) == 1:
            arrived(gath.at[m, at], gc_sem.at[m, j, 0], {"cell": cell_at(m)})
        else:
            for h, step in ((0, 1 << (m.bit_length() - 1)), (1, m & -m)):
                part = pl.ds(h * half, half)
                arrived(gath.at[m, at, part], gc_sem.at[m, j, h], {"cell": cell_at(step)})

    width = tile_of(out_ref.shape[1], 512)
    side_rows = nt // 2

    def multiply(parts, far, cols):
        top = zz // (nz // 2)
        first = ((1 - top) if far else top) * side_rows
        lhs = [gath[m, pl.ds(first, side_rows)].reshape(side_rows * qb, fw) for m in parts]
        rhs = [st[m, cols, :] for m in parts]
        piece = dot_t(jnp.concatenate(lhs, axis=1), jnp.concatenate(rhs, axis=1))
        out_ref[pl.ds(pl.multiple_of(first * qb, 128), side_rows * qb), cols] = piece

    def from_sibling(m, j):
        arrived(gath.at[m, z_at(j) + 1 - 2 * core], gs_sem.at[m, j], to_sib)

    ones = [m for m in slots if order(m) == 1]
    more = [m for m in slots if order(m) > 1]
    base = [0, *ones]
    tiles = out_ref.shape[1] // width
    units = [(far, n) for far in range(2) for n in range(tiles)]

    def run(count):
        for far, n in units[:count]:
            if n == 0:
                for m in base:
                    if not far:
                        st_loads[m].wait()
                    for j in range(far * (nz // 2), (far + 1) * (nz // 2)):
                        from_sibling(m, j)
            multiply(base, far, pl.ds(n * width, width))
        del units[:count]

    for j in range(1, nz):
        send(gath.at[0, tok], gath.at[0, tok], gz_sem.at[j], {"tok": z_at(j)})
    forward(0, 0)
    def pass_on(group, j):
        for m in group:
            take(m, j)
            forward(m, j)

    taken = 0
    for j in range(1, nz):
        pass_on(ones, j - 1)
        if j > nz // 2:
            pass_on(more, taken)
            taken += 1
        at = z_at(j)
        arrived(gath.at[0, at], gz_sem.at[j], {"tok": at})
        forward(0, j)
        if j >= nz // 2:
            run(1)
    pass_on(ones, nz - 1)
    while taken < nz:
        pass_on(more, taken)
        taken += 1
        if taken < nz:
            run(1)
    run(len(units))
    for m in more:
        st_loads[m].wait()
        for j in range(nz):
            from_sibling(m, j)

    @pl.loop(0, tiles)
    def _(n):
        cols = pl.ds(pl.multiple_of(n * width, width), width)
        for m in more:
            out_ref[:, cols] += dot_t(gath[m].reshape(Q, fw), st[m, cols, :])

    for copy in sent:
        copy.wait_send()


def shards(nt, nc, activations, out_grads, query_ids, live, proj_in, proj_out, whitener, stores):
    toks, d = activations.shape
    kv, rb = proj_out.shape
    ra = proj_in.shape[1]
    fc, feat = whitener.shape
    fw = feat // nc
    n_stores = stores.shape[0]
    nz = nt // CORES
    qb = Q // nt
    hbm = pl.BlockSpec(memory_space=pltpu.HBM)
    vmem = pl.BlockSpec(memory_space=pltpu.VMEM)
    n_loads = 5 + 2 * (toks // tile_of(toks, 256)) + 2 * nc
    dma = pltpu.SemaphoreType.DMA
    return pl.pallas_call(
        functools.partial(kernel, nt, nc),
        out_shape=pltpu.VMEM((Q, n_stores), F32),
        in_specs=[
            hbm, hbm, hbm, pl.BlockSpec(memory_space=pltpu.SMEM),
            hbm, hbm, hbm, hbm,
        ],
        out_specs=vmem,
        scratch_shapes=[
            pltpu.VMEM((toks, d), BF16),
            pltpu.VMEM((toks, kv), BF16),
            pltpu.VMEM((1, toks), jnp.int32),
            pltpu.VMEM((2, ra, d), BF16),
            pltpu.VMEM((2, rb, kv), BF16),
            pltpu.VMEM((nc, fc, fw), BF16),
            pltpu.VMEM((nc, n_stores, fw), BF16),
            pltpu.VMEM((toks, fc), BF16),
            pltpu.VMEM((2, nz * qb, toks), BF16),
            pltpu.VMEM((nz, qb, fc), BF16),
            pltpu.VMEM((nz, qb, fc), BF16),
            pltpu.VMEM((nz, qb, fc), F32),
            pltpu.VMEM((nz, qb, fc), BF16),
            pltpu.VMEM((nz, qb, fc), BF16),
            pltpu.VMEM((qb, fc), BF16),
            pltpu.VMEM((nc, qb, fw), BF16),
            pltpu.VMEM((nc, qb, fw), BF16),
            pltpu.VMEM((qb, fw), F32),
            pltpu.VMEM((nc, nt, qb, fw), BF16),
            dma((n_loads,)),
            dma((nz, 2)),
            dma((nz, 2)),
            dma((nc, 2)),
            dma((nz, 2)),
            dma((nc, nz, 2, 2)),
            dma((nc, nz, 2)),
        ],
        compiler_params=pltpu.CompilerParams(
            collective_id=0, has_side_effects=True, vmem_limit_bytes=60 * 2**20
        ),
        cost_estimate=pl.CostEstimate(
            flops=2 * Q * n_stores * feat, bytes_accessed=24 * 2**20, transcendentals=0
        ),
        name="influence_scores",
    )(activations, out_grads, query_ids.reshape(1, toks), live, proj_in.T, proj_out.T, whitener, stores)


def solution(mesh):
    in_specs = (
        P("tok", None),
        P("tok", None),
        P("tok"),
        P("tok"),
        P(None, "cell"),
        P(),
        P("cell", None),
        P(("tok", "cell"), None),
    )
    out_specs = P(None, ("tok", "cell"))
    body = functools.partial(shards, mesh.shape["tok"], mesh.shape["cell"])
    return jax.shard_map(body, mesh=mesh, in_specs=in_specs, out_specs=out_specs, check_vma=False)
```

```python
import functools

import jax
import jax.numpy as jnp
from jax import lax
from jax.experimental import pallas as pl
from jax.experimental.pallas import tpu as pltpu
from jax.sharding import PartitionSpec as P

Q = 512
CORES = 2
MESH = pl.DeviceIdType.MESH
F32 = jnp.float32
BF16 = jnp.bfloat16


def tile_of(extent, most):
    size = min(extent, most)
    while extent % size:
        size //= 2
    return size


def dot(a, b):
    return jnp.dot(a, b, preferred_element_type=F32)


def dot_t(a, b):
    return lax.dot_general(a, b, (((1,), (1,)), ((), ())), preferred_element_type=F32)


def spread(twice, pattern):
    high = twice.astype(BF16).astype(F32)
    lane = lax.broadcasted_iota(jnp.int32, twice.shape, 1)
    return dot(jnp.where(lane < twice.shape[1] // 2, high, twice - high).astype(BF16), pattern)


def flipped(index, m):
    other = index
    for k in range(m.bit_length()):
        if m & (1 << k):
            other = other + (1 << k) * (1 - 2 * ((index // (1 << k)) % 2))
    return other


def kernel(
    nt, nc, act_hbm, og_hbm, ids_hbm, live_ref, pin_hbm, pout_hbm, wh_hbm, st_hbm, out_ref,
    act, og, ids_ref, pin, pout, wh, st, st_t, outer, hot, sib_out, sib_in, own, z_out, z_in, summed, c_out, c_in, own_w, gath,
    load_sem, sib_sem, z_sem, c_sem, gz_sem, gc_sem, gs_sem,
):
    tok = lax.axis_index("tok")
    cell = lax.axis_index("cell")
    nz = nt // CORES
    zz = tok // CORES
    core = tok % CORES
    toks, fc = outer.shape
    qb = Q // nt
    fw = wh.shape[2]
    ra, rb = pin.shape[1], pout.shape[1]

    def cell_at(m):
        return flipped(cell, m)

    def z_at(j):
        return flipped(zz, j) * CORES + core

    sibling = zz * CORES + (1 - core)

    barrier = pltpu.get_barrier_semaphore()
    pl.semaphore_signal(barrier, inc=1, device_id={"tok": sibling}, device_id_type=MESH)
    for j in range(1, nz):
        pl.semaphore_signal(barrier, inc=1, device_id={"tok": z_at(j)}, device_id_type=MESH)
    for m in range(1, nc):
        pl.semaphore_signal(barrier, inc=1, device_id={"cell": cell_at(m)}, device_id_type=MESH)

    rows = tile_of(toks, 256)
    steps = toks // rows
    loads = []

    def load(src, dst):
        copy = pltpu.make_async_copy(src, dst, load_sem.at[len(loads)])
        copy.start()
        loads.append(copy)
        return copy

    ids_load = load(ids_hbm, ids_ref)
    small_loads = [load(src, dst.at[n]) for src, dst in ((pin_hbm, pin), (pout_hbm, pout)) for n in range(2)]
    chunk_loads = []
    for s in range(steps):
        part = pl.ds(s * rows, rows)
        chunk_loads.append((load(og_hbm.at[part], og.at[part]), load(act_hbm.at[part], act.at[part])))
    wh_loads, st_loads = [], []
    for m in range(nc):
        cols = pl.ds(pl.multiple_of(cell_at(m) * fw, fw), fw)
        wh_loads.append(load(wh_hbm.at[:, cols], wh.at[m]))

    ids_load.wait()
    ids = ids_ref[...]
    valid = lax.broadcasted_iota(jnp.int32, (1, toks), 1) < live_ref[0]
    ids = jnp.where(valid, ids, -1)
    row = lax.broadcasted_iota(jnp.int32, (qb, toks), 0)
    for side in range(2):
        parity = 1 - core if side == 0 else core
        for j in range(nz):
            first = (flipped(zz, j) * CORES + parity) * qb
            hot[side, pl.ds(j * qb, qb), :] = (row + first == ids).astype(F32).astype(BF16)

    def pattern(n, test):
        feat = lax.broadcasted_iota(jnp.int32, (2 * n, fc), 1)
        at = lax.broadcasted_iota(jnp.int32, (2 * n, fc), 0)
        return test(feat, jnp.where(at < n, at, at - n)).astype(F32).astype(BF16)

    left_pat = pattern(ra, lambda feat, at: (feat >= at * rb) & (feat < at * rb + rb))
    right_pat = pattern(rb, lambda feat, at: jnp.bitwise_and(feat, rb - 1) == at)

    for copy in small_loads:
        copy.wait()
    pin_twice = pin[...].reshape(2 * ra, pin.shape[2])
    pout_twice = pout[...].reshape(2 * rb, pout.shape[2])
    for s in range(steps):
        part = pl.ds(s * rows, rows)
        chunk_loads[s][0].wait()
        right = dot_t(og[part, :], pout_twice)
        chunk_loads[s][1].wait()
        left = dot_t(act[part, :], pin_twice)
        outer[part, :] = (spread(left, left_pat) * spread(right, right_pat)).astype(BF16)

    for m in range(nc):
        cols = pl.ds(pl.multiple_of(cell_at(m) * fw, fw), fw)
        st_loads.append(load(st_hbm.at[:, cols], st.at[m]))

    sent = []

    def send(src, dst, sems, where):
        copy = pltpu.make_async_remote_copy(
            src_ref=src, dst_ref=dst, send_sem=sems.at[0], recv_sem=sems.at[1],
            device_id=where, device_id_type=MESH,
        )
        copy.start()
        sent.append(copy)

    def arrived(ref, sems, where):
        pltpu.make_async_remote_copy(
            src_ref=ref, dst_ref=ref, send_sem=sems.at[0], recv_sem=sems.at[1],
            device_id=where, device_id_type=MESH,
        ).wait_recv()

    to_sib = {"tok": sibling}

    z_order = [*range(1, nz), 0]
    theirs = dot(hot[0], outer[...]).astype(BF16)
    for j in range(nz):
        sib_out[j] = theirs[j * qb : (j + 1) * qb]
    pl.semaphore_wait(barrier, 1 + (nz - 1) + (nc - 1))
    for j in z_order:
        send(sib_out.at[j], sib_in.at[j], sib_sem.at[j], to_sib)
    mine = dot(hot[1], outer[...])
    for j in range(nz):
        own[j] = mine[j * qb : (j + 1) * qb]
    for j in z_order:
        arrived(sib_in.at[j], sib_sem.at[j], to_sib)
        both = own[j] + sib_in[j].astype(F32)
        if j:
            z_out[j] = both.astype(BF16)
            send(z_out.at[j], z_in.at[j], z_sem.at[j], {"tok": z_at(j)})
        else:
            own[0] = both
    width = tile_of(out_ref.shape[1], 512)
    tiles = out_ref.shape[1] // width

    def turn(parts):
        for m in parts:
            st_loads[m].wait()

        @pl.loop(0, tiles)
        def _(n):
            cols = pl.ds(pl.multiple_of(n * width, width), width)
            for m in parts:
                st_t[m, :, cols] = st[m, cols, :].T

    early = [*range(nc - 1)]
    turn(early)
    total = own[0]
    for j in range(1, nz):
        arrived(z_in.at[j], z_sem.at[j], {"tok": z_at(j)})
        total = total + z_in[j].astype(F32)
    summed[...] = total.astype(BF16)

    for m in reversed(range(nc)):
        wh_loads[m].wait()
        product = dot(summed[...], wh[m])
        if m:
            c_out[m] = product.astype(BF16)
            send(c_out.at[m], c_in.at[m], c_sem.at[m], {"cell": cell_at(m)})
        else:
            own_w[...] = product
    turn([m for m in range(nc) if m not in early])
    total = own_w[...]
    for m in range(1, nc):
        arrived(c_in.at[m], c_sem.at[m], {"cell": cell_at(m)})
        total = total + c_in[m].astype(F32)
    gath[0, tok] = total.astype(BF16)

    half = qb // 2

    def order(m):
        return bin(m).count("1")

    slots = sorted(range(nc), key=order)

    def forward(s, j):
        at = z_at(j)
        for m in slots:
            if order(m) != order(s) + 1 or (m & s) != s:
                continue
            step = m ^ s
            where = {"cell": cell_at(step)}
            if order(m) == 1:
                send(gath.at[s, at], gath.at[m, at], gc_sem.at[m, j, 0], where)
                continue
            if step == 1 << (m.bit_length() - 1):
                part = pl.ds(0, half)
                send(gath.at[s, at, part], gath.at[m, at, part], gc_sem.at[m, j, 0], where)
            if step == m & -m:
                part = pl.ds(half, half)
                send(gath.at[s, at, part], gath.at[m, at, part], gc_sem.at[m, j, 1], where)
        send(gath.at[s, at], gath.at[s, at], gs_sem.at[s, j], to_sib)

    def take(m, j):
        at = z_at(j)
        if order(m) == 1:
            arrived(gath.at[m, at], gc_sem.at[m, j, 0], {"cell": cell_at(m)})
        else:
            for h, step in ((0, 1 << (m.bit_length() - 1)), (1, m & -m)):
                part = pl.ds(h * half, half)
                arrived(gath.at[m, at, part], gc_sem.at[m, j, h], {"cell": cell_at(step)})

    side_rows = nt // 2

    def multiply(parts, far, cols):
        top = zz // (nz // 2)
        first = ((1 - top) if far else top) * side_rows
        lhs = [gath[m, pl.ds(first, side_rows)].reshape(side_rows * qb, fw) for m in parts]
        rhs = [st_t[m, :, cols] for m in parts]
        piece = dot(jnp.concatenate(lhs, axis=1), jnp.concatenate(rhs, axis=0))
        out_ref[pl.ds(pl.multiple_of(first * qb, 128), side_rows * qb), cols] = piece

    def from_sibling(m, j):
        arrived(gath.at[m, z_at(j) + 1 - 2 * core], gs_sem.at[m, j], to_sib)

    ones = [m for m in slots if order(m) == 1]
    more = [m for m in slots if order(m) > 1]
    base = [0, *ones]
    units = [(far, n) for far in range(2) for n in range(tiles)]

    def run(count):
        for far, n in units[:count]:
            if n == 0:
                for m in base:
                    for j in range(far * (nz // 2), (far + 1) * (nz // 2)):
                        from_sibling(m, j)
            multiply(base, far, pl.ds(n * width, width))
        del units[:count]

    for j in range(1, nz):
        send(gath.at[0, tok], gath.at[0, tok], gz_sem.at[j], {"tok": z_at(j)})
    forward(0, 0)
    def pass_on(group, j):
        for m in group:
            take(m, j)
            forward(m, j)

    taken = 0
    for j in range(1, nz):
        pass_on(ones, j - 1)
        if j > nz // 2:
            pass_on(more, taken)
            taken += 1
        at = z_at(j)
        arrived(gath.at[0, at], gz_sem.at[j], {"tok": at})
        forward(0, j)
        if j >= nz // 2:
            run(1)
    pass_on(ones, nz - 1)
    while taken < nz:
        pass_on(more, taken)
        taken += 1
        if taken < nz:
            run(1)
    run(len(units))
    for m in more:
        for j in range(nz):
            from_sibling(m, j)

    @pl.loop(0, tiles)
    def _(n):
        cols = pl.ds(pl.multiple_of(n * width, width), width)
        for m in more:
            out_ref[:, cols] += dot(gath[m].reshape(Q, fw), st_t[m, :, cols])

    for copy in sent:
        copy.wait_send()


def shards(nt, nc, activations, out_grads, query_ids, live, proj_in, proj_out, whitener, stores):
    toks, d = activations.shape
    kv, rb = proj_out.shape
    ra = proj_in.shape[1]
    fc, feat = whitener.shape
    fw = feat // nc
    n_stores = stores.shape[0]
    nz = nt // CORES
    qb = Q // nt
    hbm = pl.BlockSpec(memory_space=pltpu.HBM)
    vmem = pl.BlockSpec(memory_space=pltpu.VMEM)
    n_loads = 5 + 2 * (toks // tile_of(toks, 256)) + 2 * nc
    dma = pltpu.SemaphoreType.DMA
    return pl.pallas_call(
        functools.partial(kernel, nt, nc),
        out_shape=pltpu.VMEM((Q, n_stores), F32),
        in_specs=[
            hbm, hbm, hbm, pl.BlockSpec(memory_space=pltpu.SMEM),
            hbm, hbm, hbm, hbm,
        ],
        out_specs=vmem,
        scratch_shapes=[
            pltpu.VMEM((toks, d), BF16),
            pltpu.VMEM((toks, kv), BF16),
            pltpu.VMEM((1, toks), jnp.int32),
            pltpu.VMEM((2, ra, d), BF16),
            pltpu.VMEM((2, rb, kv), BF16),
            pltpu.VMEM((nc, fc, fw), BF16),
            pltpu.VMEM((nc, n_stores, fw), BF16),
            pltpu.VMEM((nc, fw, n_stores), BF16),
            pltpu.VMEM((toks, fc), BF16),
            pltpu.VMEM((2, nz * qb, toks), BF16),
            pltpu.VMEM((nz, qb, fc), BF16),
            pltpu.VMEM((nz, qb, fc), BF16),
            pltpu.VMEM((nz, qb, fc), F32),
            pltpu.VMEM((nz, qb, fc), BF16),
            pltpu.VMEM((nz, qb, fc), BF16),
            pltpu.VMEM((qb, fc), BF16),
            pltpu.VMEM((nc, qb, fw), BF16),
            pltpu.VMEM((nc, qb, fw), BF16),
            pltpu.VMEM((qb, fw), F32),
            pltpu.VMEM((nc, nt, qb, fw), BF16),
            dma((n_loads,)),
            dma((nz, 2)),
            dma((nz, 2)),
            dma((nc, 2)),
            dma((nz, 2)),
            dma((nc, nz, 2, 2)),
            dma((nc, nz, 2)),
        ],
        compiler_params=pltpu.CompilerParams(
            collective_id=0, has_side_effects=True, vmem_limit_bytes=60 * 2**20
        ),
        cost_estimate=pl.CostEstimate(
            flops=2 * Q * n_stores * feat, bytes_accessed=24 * 2**20, transcendentals=0
        ),
        name="influence_scores",
    )(activations, out_grads, query_ids.reshape(1, toks), live, proj_in.T, proj_out.T, whitener, stores)


def solution(mesh):
    in_specs = (
        P("tok", None),
        P("tok", None),
        P("tok"),
        P("tok"),
        P(None, "cell"),
        P(),
        P("cell", None),
        P(("tok", "cell"), None),
    )
    out_specs = P(None, ("tok", "cell"))
    body = functools.partial(shards, mesh.shape["tok"], mesh.shape["cell"])
    return jax.shard_map(body, mesh=mesh, in_specs=in_specs, out_specs=out_specs, check_vma=False)
```

```python
import functools

import jax
import jax.numpy as jnp
from jax import lax
from jax.experimental import pallas as pl
from jax.experimental.pallas import tpu as pltpu
from jax.sharding import PartitionSpec as P

Q = 512
CORES = 2
MESH = pl.DeviceIdType.MESH
F32 = jnp.float32
BF16 = jnp.bfloat16


def tile_of(extent, most):
    size = min(extent, most)
    while extent % size:
        size //= 2
    return size


def dot(a, b):
    return jnp.dot(a, b, preferred_element_type=F32)


def dot_t(a, b):
    return lax.dot_general(a, b, (((1,), (1,)), ((), ())), preferred_element_type=F32)


def spread(twice, pattern):
    high = twice.astype(BF16).astype(F32)
    lane = lax.broadcasted_iota(jnp.int32, twice.shape, 1)
    return dot(jnp.where(lane < twice.shape[1] // 2, high, twice - high).astype(BF16), pattern)


def kernel(
    nt, nc, act_hbm, og_hbm, ids_hbm, live_ref, pin_hbm, pout_hbm, wh_hbm, st_hbm, out_ref,
    act, og, ids_ref, pin, pout, wh, st, outer, hot, sib_out, sib_in, own, z_out, z_in, summed, c_out, c_in, own_w, gath,
    load_sem, sib_sem, z_sem, c_sem, gz_sem, gc_sem, gs_sem,
):
    tok = lax.axis_index("tok")
    cell = lax.axis_index("cell")
    nz = nt // CORES
    zz = tok // CORES
    core = tok % CORES
    toks, fc = outer.shape
    qb = Q // nt
    fw = wh.shape[2]
    ra, rb = pin.shape[1], pout.shape[1]
    bits = nc.bit_length() - 1

    def cell_at(m):
        other = cell
        for k in range(bits):
            if m & (1 << k):
                other = other + (1 << k) * (1 - 2 * ((cell // (1 << k)) % 2))
        return other

    def z_at(j):
        return ((zz + j) % nz) * CORES + core

    def z_from(j):
        return ((zz + nz - j) % nz) * CORES

    sibling = zz * CORES + (1 - core)

    barrier = pltpu.get_barrier_semaphore()
    pl.semaphore_signal(barrier, inc=1, device_id={"tok": sibling}, device_id_type=MESH)
    for j in range(1, nz):
        pl.semaphore_signal(barrier, inc=1, device_id={"tok": z_at(j)}, device_id_type=MESH)
    for m in range(1, nc):
        pl.semaphore_signal(barrier, inc=1, device_id={"cell": cell_at(m)}, device_id_type=MESH)

    rows = tile_of(toks, 256)
    steps = toks // rows
    loads = []

    def load(src, dst):
        copy = pltpu.make_async_copy(src, dst, load_sem.at[len(loads)])
        copy.start()
        loads.append(copy)
        return copy

    ids_load = load(ids_hbm, ids_ref)
    small_loads = [load(src, dst.at[n]) for src, dst in ((pin_hbm, pin), (pout_hbm, pout)) for n in range(2)]
    chunk_loads = []
    for s in range(steps):
        part = pl.ds(s * rows, rows)
        chunk_loads.append((load(og_hbm.at[part], og.at[part]), load(act_hbm.at[part], act.at[part])))
    wh_loads, st_loads = [], []
    for m in range(nc):
        cols = pl.ds(pl.multiple_of(cell_at(m) * fw, fw), fw)
        wh_loads.append(load(wh_hbm.at[:, cols], wh.at[m]))

    ids_load.wait()
    ids = ids_ref[...]
    valid = lax.broadcasted_iota(jnp.int32, (1, toks), 1) < live_ref[0]
    ids = jnp.where(valid, ids, -1)
    row = lax.broadcasted_iota(jnp.int32, (qb, toks), 0)
    for side in range(2):
        parity = 1 - core if side == 0 else core
        for j in range(nz):
            first = (((zz + j) % nz) * CORES + parity) * qb
            hot[side, pl.ds(j * qb, qb), :] = (row + first == ids).astype(F32).astype(BF16)

    def pattern(n, test):
        feat = lax.broadcasted_iota(jnp.int32, (2 * n, fc), 1)
        at = lax.broadcasted_iota(jnp.int32, (2 * n, fc), 0)
        return test(feat, jnp.where(at < n, at, at - n)).astype(F32).astype(BF16)

    left_pat = pattern(ra, lambda feat, at: (feat >= at * rb) & (feat < at * rb + rb))
    right_pat = pattern(rb, lambda feat, at: jnp.bitwise_and(feat, rb - 1) == at)

    for copy in small_loads:
        copy.wait()
    pin_twice = pin[...].reshape(2 * ra, pin.shape[2])
    pout_twice = pout[...].reshape(2 * rb, pout.shape[2])
    for s in range(steps):
        part = pl.ds(s * rows, rows)
        chunk_loads[s][0].wait()
        right = dot_t(og[part, :], pout_twice)
        chunk_loads[s][1].wait()
        left = dot_t(act[part, :], pin_twice)
        outer[part, :] = (spread(left, left_pat) * spread(right, right_pat)).astype(BF16)

    for m in range(nc):
        cols = pl.ds(pl.multiple_of(cell_at(m) * fw, fw), fw)
        st_loads.append(load(st_hbm.at[:, cols], st.at[m]))

    sent = []

    def send(src, dst, sems, where):
        copy = pltpu.make_async_remote_copy(
            src_ref=src, dst_ref=dst, send_sem=sems.at[0], recv_sem=sems.at[1],
            device_id=where, device_id_type=MESH,
        )
        copy.start()
        sent.append(copy)

    def arrived(ref, sems, where):
        pltpu.make_async_remote_copy(
            src_ref=ref, dst_ref=ref, send_sem=sems.at[0], recv_sem=sems.at[1],
            device_id=where, device_id_type=MESH,
        ).wait_recv()

    to_sib = {"tok": sibling}

    z_order = [*range(1, nz), 0]
    theirs = dot(hot[0], outer[...]).astype(BF16)
    for j in range(nz):
        sib_out[j] = theirs[j * qb : (j + 1) * qb]
    pl.semaphore_wait(barrier, 1 + (nz - 1) + (nc - 1))
    for j in z_order:
        send(sib_out.at[j], sib_in.at[j], sib_sem.at[j], to_sib)
    mine = dot(hot[1], outer[...])
    for j in range(nz):
        own[j] = mine[j * qb : (j + 1) * qb]
    for j in z_order:
        arrived(sib_in.at[j], sib_sem.at[j], to_sib)
        both = own[j] + sib_in[j].astype(F32)
        if j:
            z_out[j] = both.astype(BF16)
            send(z_out.at[j], z_in.at[j], z_sem.at[j], {"tok": z_at(j)})
        else:
            own[0] = both
    total = own[0]
    for j in range(1, nz):
        arrived(z_in.at[j], z_sem.at[j], {"tok": z_at(j)})
        total = total + z_in[j].astype(F32)
    summed[...] = total.astype(BF16)

    for m in reversed(range(nc)):
        wh_loads[m].wait()
        product = dot(summed[...], wh[m])
        if m:
            c_out[m] = product.astype(BF16)
            send(c_out.at[m], c_in.at[m], c_sem.at[m], {"cell": cell_at(m)})
        else:
            own_w[...] = product
    total = own_w[...]
    for m in range(1, nc):
        arrived(c_in.at[m], c_sem.at[m], {"cell": cell_at(m)})
        total = total + c_in[m].astype(F32)
    gath[0, tok] = total.astype(BF16)

    half = qb // 2

    def order(m):
        return bin(m).count("1")

    slots = sorted(range(nc), key=order)

    def forward(s, j):
        at = z_from(j) + core
        for m in slots:
            if order(m) != order(s) + 1 or (m & s) != s:
                continue
            step = m ^ s
            where = {"cell": cell_at(step)}
            if order(m) == 1:
                send(gath.at[s, at], gath.at[m, at], gc_sem.at[m, j, 0], where)
                continue
            if step == 1 << (m.bit_length() - 1):
                part = pl.ds(0, half)
                send(gath.at[s, at, part], gath.at[m, at, part], gc_sem.at[m, j, 0], where)
            if step == m & -m:
                part = pl.ds(half, half)
                send(gath.at[s, at, part], gath.at[m, at, part], gc_sem.at[m, j, 1], where)
        send(gath.at[s, at], gath.at[s, at], gs_sem.at[s, j], to_sib)

    def take(m, j):
        at = z_from(j) + core
        if order(m) == 1:
            arrived(gath.at[m, at], gc_sem.at[m, j, 0], {"cell": cell_at(m)})
        else:
            for h, step in ((0, 1 << (m.bit_length() - 1)), (1, m & -m)):
                part = pl.ds(h * half, half)
                arrived(gath.at[m, at, part], gc_sem.at[m, j, h], {"cell": cell_at(step)})

    def multiply(m):
        for j in range(nz):
            at = z_from(j) + (1 - core)
            arrived(gath.at[m, at], gs_sem.at[m, j], to_sib)
        st_loads[m].wait()
        width = tile_of(out_ref.shape[1], 512)

        @pl.loop(0, out_ref.shape[1] // width)
        def _(n):
            cols = pl.ds(pl.multiple_of(n * width, width), width)
            piece = dot_t(gath[m].reshape(Q, fw), st[m, cols, :])
            if m == 0:
                out_ref[:, cols] = piece
            else:
                out_ref[:, cols] += piece

    for j in range(1, nz):
        send(gath.at[0, tok], gath.at[0, tok], gz_sem.at[j], {"tok": z_at(j)})
    forward(0, 0)
    ones = [m for m in slots if order(m) == 1]
    more = [m for m in slots if order(m) > 1]
    for j in range(1, nz):
        for m in ones:
            take(m, j - 1)
            forward(m, j - 1)
        at = z_from(j) + core
        arrived(gath.at[0, at], gz_sem.at[j], {"tok": at})
        forward(0, j)
    multiply(0)
    for m in ones:
        take(m, nz - 1)
        forward(m, nz - 1)
    todo = list(ones)
    for m in more:
        for j in range(nz):
            take(m, j)
            forward(m, j)
            if todo and j >= nz // 2 - 1 and j < nz - 1:
                multiply(todo.pop(0))
        todo.append(m)
    for m in todo:
        multiply(m)
    for copy in sent:
        copy.wait_send()


def shards(nt, nc, activations, out_grads, query_ids, live, proj_in, proj_out, whitener, stores):
    toks, d = activations.shape
    kv, rb = proj_out.shape
    ra = proj_in.shape[1]
    fc, feat = whitener.shape
    fw = feat // nc
    n_stores = stores.shape[0]
    nz = nt // CORES
    qb = Q // nt
    hbm = pl.BlockSpec(memory_space=pltpu.HBM)
    vmem = pl.BlockSpec(memory_space=pltpu.VMEM)
    n_loads = 5 + 2 * (toks // tile_of(toks, 256)) + 2 * nc
    dma = pltpu.SemaphoreType.DMA
    return pl.pallas_call(
        functools.partial(kernel, nt, nc),
        out_shape=pltpu.VMEM((Q, n_stores), F32),
        in_specs=[
            hbm, hbm, hbm, pl.BlockSpec(memory_space=pltpu.SMEM),
            hbm, hbm, hbm, hbm,
        ],
        out_specs=vmem,
        scratch_shapes=[
            pltpu.VMEM((toks, d), BF16),
            pltpu.VMEM((toks, kv), BF16),
            pltpu.VMEM((1, toks), jnp.int32),
            pltpu.VMEM((2, ra, d), BF16),
            pltpu.VMEM((2, rb, kv), BF16),
            pltpu.VMEM((nc, fc, fw), BF16),
            pltpu.VMEM((nc, n_stores, fw), BF16),
            pltpu.VMEM((toks, fc), BF16),
            pltpu.VMEM((2, nz * qb, toks), BF16),
            pltpu.VMEM((nz, qb, fc), BF16),
            pltpu.VMEM((nz, qb, fc), BF16),
            pltpu.VMEM((nz, qb, fc), F32),
            pltpu.VMEM((nz, qb, fc), BF16),
            pltpu.VMEM((nz, qb, fc), BF16),
            pltpu.VMEM((qb, fc), BF16),
            pltpu.VMEM((nc, qb, fw), BF16),
            pltpu.VMEM((nc, qb, fw), BF16),
            pltpu.VMEM((qb, fw), F32),
            pltpu.VMEM((nc, nt, qb, fw), BF16),
            dma((n_loads,)),
            dma((nz, 2)),
            dma((nz, 2)),
            dma((nc, 2)),
            dma((nz, 2)),
            dma((nc, nz, 2, 2)),
            dma((nc, nz, 2)),
        ],
        compiler_params=pltpu.CompilerParams(
            collective_id=0, has_side_effects=True, vmem_limit_bytes=60 * 2**20
        ),
        cost_estimate=pl.CostEstimate(
            flops=2 * Q * n_stores * feat, bytes_accessed=24 * 2**20, transcendentals=0
        ),
        name="influence_scores",
    )(activations, out_grads, query_ids.reshape(1, toks), live, proj_in.T, proj_out.T, whitener, stores)


def solution(mesh):
    in_specs = (
        P("tok", None),
        P("tok", None),
        P("tok"),
        P("tok"),
        P(None, "cell"),
        P(),
        P("cell", None),
        P(("tok", "cell"), None),
    )
    out_specs = P(None, ("tok", "cell"))
    body = functools.partial(shards, mesh.shape["tok"], mesh.shape["cell"])
    return jax.shard_map(body, mesh=mesh, in_specs=in_specs, out_specs=out_specs, check_vma=False)
```
